256 devices in a mesh: slab: 4 (over z_lo), tile: 64 (over y, z_hi, x, core).
Axes of the slice: x: 4, y: 4, z: 8 (z_hi: 2, z_lo: 4; z = z_hi * 4 + z_lo), core: 2. Of those that a mesh axis runs over, the one named last changes fastest.
Arguments:
- features: bfloat16 [2048, 64, 512], P(('slab', 'tile')), may hold values from -6 to 6
- cotangent: bfloat16 [2048, 64, 512], P(('slab', 'tile')), may hold values from -6 to 6
- weight: bfloat16 [64, 1728], replicated, may hold values from -0.15625 to 0.15625
- block_table: int32 [4, 128, 8], replicated, may hold values from -1 to 7, as said below
Outputs:
- conv_out: bfloat16 [2048, 64, 512], P(('slab', 'tile'))
- grad_features: bfloat16 [2048, 64, 512], P(('slab', 'tile'))
- grad_weight: float32 [64, 1728], replicated
The draws below stay inside these ranges and needn't reach their ends.
Inputs may be any that keep to these rules, and one draw needn't show every extreme that they name: `block_table`: -1 marks an inactive block. An active block (bz, by, bx) holds (by modulo 2) * 4 plus the number of active blocks before it along x in its row (bz, by). Every row has at least one and at most 4 active blocks; all rows of one block layer bz share an active block in one column. Some row with by modulo 2 = 1 has exactly 4.
All inputs are finite; a program needn't handle non-finite values.
Results may differ from the reference program's by a relative error of at most 0.001.
Values may be sent and summed in bfloat16 or wider, within the bound.
No kernel may reach another device: no remote copies, remote signals or barrier semaphores. Data moves between devices by JAX's collectives and lax.ppermute only.
A program may use at most 64 MiB of HBM per device.

```python
import jax
import jax.numpy as jnp
from jax import lax

CH = 64
LZ = 1
YR = 2
LX = 8
CAPL = 4
BLOCKS = 2048
ZBLOCKS = 4
YBLOCKS = 128
N_TILE = 64


def draw_block_table(key, part):
    row_count = ZBLOCKS * YBLOCKS
    key_count, key_slab, key_tile, key_order, key_column = jax.random.split(key, 5)
    counts = jax.random.randint(key_count, (row_count,), 1, CAPL + 1)
    full_slab = jax.random.randint(key_slab, (), 0, ZBLOCKS // LZ)
    full_tile = jax.random.randint(key_tile, (), 0, YBLOCKS // YR)
    full_row = (full_slab * LZ + LZ - 1) * YBLOCKS + full_tile * YR + YR - 1
    row_ids = jnp.arange(row_count).astype(jnp.int32)
    counts = jnp.where(row_ids == full_row, CAPL, counts)
    order_keys = jax.random.split(key_order, row_count)
    ranking = jax.vmap(lambda row_key: jax.random.permutation(row_key, LX))(order_keys)
    layer_column = jax.random.randint(key_column, (ZBLOCKS,), 0, LX)
    row_column = layer_column[row_ids // YBLOCKS]
    positions = jnp.arange(LX).astype(jnp.int32)
    rank_there = jnp.sum(jnp.where(positions[None, :] == row_column[:, None], ranking, 0), axis=1)
    lifted = jnp.where(ranking < rank_there[:, None], ranking + 1, ranking)
    ranking = jnp.where(positions[None, :] == row_column[:, None], 0, lifted)
    active = (ranking < counts[:, None]).astype(jnp.int32)
    within = jnp.cumsum(active, axis=1) - 1
    layer_z = row_ids // YBLOCKS % LZ
    layer_y = row_ids % YBLOCKS % YR
    base_value = (layer_z * YR + layer_y) * CAPL
    table = jnp.where(active > 0, base_value[:, None] + within, -1)
    return table.reshape(ZBLOCKS, YBLOCKS, LX).astype(jnp.int32)


def shard_levels(stream_key, extent, pieces, least, top_value):
    def one(axis_at, shards_of):
        draws = jax.random.uniform(jax.random.fold_in(jax.random.fold_in(stream_key, 6), axis_at), (shards_of,), jnp.float32, least / len(pieces), top_value / len(pieces))
        return jnp.repeat(jnp.exp(draws), extent[axis_at] // shards_of).reshape((-1,) + (1,) * (len(extent) - axis_at - 1))

    level = one(*pieces[0])
    for cut in pieces[1:]:
        level = level * one(*cut)
    return level


def gaussian(rng, shape, width, reach, cuts=(), held_as=jnp.bfloat16):
    array = width * jax.random.normal(rng, shape, jnp.float32)
    if cuts:
        array = array * shard_levels(rng, shape, cuts, -0.22, 0.18)
    return jnp.clip(array, -reach, reach).astype(held_as)


def setup_inputs(seed: int = 0) -> dict:
    key_list = jax.random.split(jax.random.key(seed), 5)
    return {
        "features": gaussian(key_list[0], (BLOCKS, CH, 512), 1.0, 6.0, ((0, 256),)),
        "cotangent": gaussian(key_list[1], (BLOCKS, CH, 512), 1.0, 6.0, ((0, 256),)),
        "weight": gaussian(key_list[2], (CH, 27 * CH), (27 * CH) ** -0.5, 0.15625),
        "block_table": draw_block_table(jax.random.fold_in(key_list[4], 71), 0),
    }


def neighbours(block_table):
    capacity = LZ * YR * CAPL
    row_ids = jnp.arange(BLOCKS).astype(jnp.int32)
    device_ids = row_ids // capacity
    slot_ids = row_ids % capacity
    z_pos = device_ids // N_TILE * LZ + slot_ids // (YR * CAPL)
    y_pos = device_ids % N_TILE * YR + slot_ids // CAPL % YR
    table_rows = block_table[z_pos, y_pos]
    matches = table_rows == slot_ids[:, None]
    positions = jnp.arange(LX).astype(jnp.int32)
    x_pos = lax.optimization_barrier(jnp.sum(jnp.where(matches, positions[None, :], 0), axis=1)).astype(jnp.int32)
    is_valid = jnp.any(matches, axis=1)
    found_lists = []
    for step_z in (-1, 0, 1):
        for step_y in (-1, 0, 1):
            for step_x in (-1, 0, 1):
                near_z = z_pos + step_z
                near_y = y_pos + step_y
                near_x = x_pos + step_x
                inside = (near_z >= 0) & (near_z < ZBLOCKS) & (near_y >= 0) & (near_y < YBLOCKS) & (near_x >= 0) & (near_x < LX)
                clip_z = jnp.clip(near_z, 0, ZBLOCKS - 1).astype(jnp.int32)
                clip_y = jnp.clip(near_y, 0, YBLOCKS - 1).astype(jnp.int32)
                clip_x = jnp.clip(near_x, 0, LX - 1).astype(jnp.int32)
                local_index = block_table[clip_z, clip_y, clip_x]
                owner = clip_z // LZ * N_TILE + clip_y // YR
                found_lists.append(jnp.where(inside & (local_index >= 0), owner * capacity + local_index, -1).astype(jnp.int32))
    return (jnp.stack(found_lists, axis=1), is_valid)

def padded_cube(volume, indices):
    keep_mask = (indices >= 0).astype(volume.dtype)
    gathered = volume[jnp.maximum(indices, 0)] * keep_mask[:, None, None, None, None]
    whole = gathered.reshape(3, 3, 3, CH, 8, 8, 8).transpose(3, 0, 4, 1, 5, 2, 6).reshape(CH, 24, 24, 24)
    return whole[:, 7:17, 7:17, 7:17]

def unfold_cube(cube_data):
    windows = [cube_data[:, from_z:from_z + 8, from_y:from_y + 8, from_x:from_x + 8] for from_z in range(3) for from_y in range(3) for from_x in range(3)]
    return jnp.stack(windows, axis=0).reshape(27 * CH, 512)

def reference(features, cotangent, weight, block_table):
    neighbour_index, is_valid = neighbours(block_table)
    volume_x = features.reshape(BLOCKS, CH, 8, 8, 8)
    volume_g = cotangent.reshape(BLOCKS, CH, 8, 8, 8)
    back_weight = jnp.transpose(weight.reshape(CH, 27, CH)[:, ::-1, :], (2, 1, 0)).reshape(CH, 27 * CH)

    def block_step(grad_weight, inputs):
        indices, valid_here, own_grad = inputs
        cols_x = unfold_cube(padded_cube(volume_x, indices))
        cols_g = unfold_cube(padded_cube(volume_g, indices))
        valid_mask = valid_here.astype(jnp.float32)
        forward_part = jnp.dot(weight, cols_x, preferred_element_type=jnp.float32) * valid_mask
        backward_part = jnp.dot(back_weight, cols_g, preferred_element_type=jnp.float32) * valid_mask
        weight_term = jnp.dot(own_grad, cols_x.T, preferred_element_type=jnp.float32) * valid_mask
        return (grad_weight + weight_term, (forward_part.astype(jnp.bfloat16), backward_part.astype(jnp.bfloat16)))
    summed, outputs = lax.scan(block_step, jnp.zeros((CH, 27 * CH), jnp.float32), (neighbour_index, is_valid, cotangent))
    voxels = jnp.sum((block_table >= 0).astype(jnp.float32)) * 512.0
    return (outputs[0], outputs[1], summed / jnp.sqrt(voxels))
```

```python
import jax
import jax.numpy as jnp
import numpy as np
from jax import lax
from jax.experimental import pallas as pl
from jax.experimental.pallas import tpu as pltpu
from jax.sharding import PartitionSpec as P

LX = 8
YR = 2
BF = jnp.bfloat16
F32 = jnp.float32
AXES = ("slab", "tile")
N_DEV = 256
VMEM_LIMIT = 48 * 1024 * 1024
SHIFTS = [dy * 10 + dx for dy in (-1, 0, 1) for dx in (-1, 0, 1)]


def params():
    return pltpu.CompilerParams(vmem_limit_bytes=VMEM_LIMIT)


def iota(shape, dim):
    return lax.broadcasted_iota(jnp.int32, shape, dim)


def halves(a, b, right):
    cut = slice(64, 128) if right else slice(0, 64)
    return jnp.concatenate([a[:, cut], b[:, cut]], axis=1)


def faces_kernel(x0_ref, x3_ref, g0_ref, g3_ref, low_ref, high_ref):
    for s in range(8):
        low_ref[s] = halves(x0_ref[s], g0_ref[s], False)
        high_ref[s] = halves(x3_ref[s], g3_ref[s], True)


def faces(x, g):
    def at(t):
        return pl.BlockSpec((8, 64, 128), lambda i, t=t: (0, 0, t))

    whole = pl.BlockSpec((8, 64, 128), lambda i: (0, 0, 0))
    face = jax.ShapeDtypeStruct((8, 64, 128), BF)
    return pl.pallas_call(
        faces_kernel,
        grid=(1,),
        in_specs=[at(0), at(3), at(0), at(3)],
        out_specs=[whole, whole],
        out_shape=[face, face],
        compiler_params=params(),
        name="faces",
    )(x, x, g, g)


def edges_kernel(core_ref, x_ref, g_ref, below_ref, above_ref, pair_ref, other_ref):
    chunk = iota((1024, 128), 0) // 128
    lane = iota((1024, 128), 0) % 128
    to = iota((1024, 128), 1)

    def picks(y):
        here = (lane // 8) % 8 == y
        edge = (lane // 64) * 64 + chunk * 8 + lane % 8
        line = (chunk // 4) * 64 + (lane // 64) * 32 + (chunk % 4) * 8 + lane % 8
        return [
            jnp.where(here & (at == to), 1.0, 0.0).astype(BF) for at in (edge, line)
        ]

    found = []
    for first, y in ((4, 7), (0, 0)):
        edge, line = picks(y)
        rows = [
            jnp.concatenate(
                [ref[first + s, :, 128 * t : 128 * t + 128] for ref in (x_ref, g_ref) for s in range(4)],
                axis=1,
            )
            for t in range(4)
        ]
        lines = jnp.concatenate(
            [ref[first + s] for ref in (below_ref, above_ref) for s in range(4)], axis=1
        )
        main = jnp.dot(jnp.concatenate(rows, axis=0), edge, preferred_element_type=F32)
        last = jnp.dot(lines, line, preferred_element_type=F32)
        found.append(jnp.concatenate([main, last], axis=0))
    up, down = found
    odd = core_ref[0]
    pair_ref[...] = jnp.where(odd == 0, up, down).astype(BF)
    other_ref[...] = jnp.where(odd == 0, down, up).astype(BF)


def edges(core, x, g, below, above):
    out = jax.ShapeDtypeStruct((320, 128), BF)
    vmem = pl.BlockSpec(memory_space=pltpu.VMEM)
    return pl.pallas_call(
        edges_kernel,
        in_specs=[pl.BlockSpec(memory_space=pltpu.SMEM)] + [vmem] * 4,
        out_specs=[vmem, vmem],
        out_shape=[out, out],
        compiler_params=params(),
        name="edges",
    )(core, x, g, below, above)


def places_kernel(core_ref, table_ref, place_ref):
    odd = core_ref[0]
    lane = iota((8, 128), 1)
    ly = lane // 10 - 1
    lx = lane % 10 - 1
    used = lane < 100
    y_class = jnp.where(ly < 0, 0, jnp.where(ly > 7, 2, 1))
    x_class = jnp.where(lx < 0, 0, jnp.where(lx > 7, 2, 1))
    near = jnp.where(used, y_class * 3 + x_class, -1)
    inner_x = lx & 7
    inner = (ly & 7) * 8 + inner_x
    rows = iota((768, 128), 0)
    for s in range(8):
        r = s // 4
        column = jnp.int32(-10)
        for b in range(8):
            column = jnp.where(table_ref[(4 + r + 1) * 8 + b] == s, b, column)
        for d in range(3):
            source = jnp.full((8, 128), -1, jnp.int32)
            for dy in range(3):
                row = r + dy
                for dx in range(3):
                    at = column + (dx - 1)
                    inside = (at >= 0) & (at < LX)
                    held = table_ref[(d * 4 + row) * 8 + jnp.clip(at, 0, LX - 1)]
                    fine = inside & (held >= 0)
                    if row in (1, 2):
                        base = jnp.where(fine, held * 64, -10000)
                        value = base + inner
                    else:
                        side = 1 - odd if row == 0 else odd
                        base = jnp.where(fine, 512 + side * 128 + (held & 3) * 8, -10000)
                        value = base + inner_x
                    source = jnp.where(near == dy * 3 + dx, value, source)
            place_ref[d, :, 128 * s : 128 * s + 128] = jnp.where(
                rows == source[0:1], 1.0, 0.0
            ).astype(BF)


def places(core, window):
    smem = pl.BlockSpec(memory_space=pltpu.SMEM)
    return pl.pallas_call(
        places_kernel,
        in_specs=[smem, smem],
        out_specs=pl.BlockSpec(memory_space=pltpu.VMEM),
        out_shape=jax.ShapeDtypeStruct((3, 768, 1024), BF),
        compiler_params=params(),
        name="places",
    )(core, window)


def taps(planes_ref, slot, z_from, z_count):
    at = pl.ds(pl.multiple_of(slot * 128, 128), 128)
    return jnp.concatenate(
        [
            jnp.concatenate(
                [planes_ref[64 * (z + dz) : 64 * (z + dz) + 64, at] for z in range(z_from, z_from + z_count)],
                axis=1,
            )
            for dz in range(3)
        ],
        axis=0,
    )


def terms_kernel(scale_ref, place_ref, x_ref, g_ref, below_ref, above_ref, pair_ref, other_ref, planes_ref, terms_ref, left_ref, total_ref):
    def fill(row, tiles, right, band, lane_group):
        for j in range(4):
            left_ref[row : row + 64, 128 * j : 128 * j + 128] = halves(tiles[2 * j], tiles[2 * j + 1], right)
        for side, ref in enumerate((pair_ref, other_ref)):
            tile = ref[64 * band : 64 * band + 64]
            if lane_group:
                tile = pltpu.roll(tile, 128 - 32 * lane_group, 1)
            left_ref[row : row + 64, 512 + 128 * side : 640 + 128 * side] = tile

    for a, ref in enumerate((x_ref, g_ref)):
        for t in range(4):
            tiles = [ref[s, :, 128 * t : 128 * t + 128] for s in range(8)]
            for parity in range(2):
                fill(512 * a + 64 * (2 * t + parity), tiles, parity, t, 2 * parity + a)
    for side, ref in enumerate((below_ref, above_ref)):
        tiles = [ref[s] for s in range(8)]
        for a in range(2):
            fill(1024 + 128 * side + 64 * a, tiles, a, 4, 2 * side + a)

    for a in range(2):
        planes_ref[640 * a + 64 : 640 * a + 576] = jnp.dot(
            left_ref[512 * a : 512 * a + 512], place_ref[1], preferred_element_type=F32
        ).astype(BF)
    for side in range(2):
        both = jnp.dot(
            left_ref[1024 + 128 * side : 1152 + 128 * side],
            place_ref[2 * side],
            preferred_element_type=F32,
        ).astype(BF)
        planes_ref[576 * side : 576 * side + 64] = both[:64]
        planes_ref[640 + 576 * side : 640 + 576 * side + 64] = both[64:]

    total_ref[...] = jnp.zeros_like(total_ref)
    lane = iota((64, 128), 1)
    column = lane % 10
    inner = (lane >= 10) & (lane < 90) & (column >= 1) & (column <= 8)

    def step(slot, carry):
        at = pl.ds(pl.multiple_of(slot * 128, 128), 128)
        own = [
            jnp.where(inner, planes_ref[640 + 64 * (z + 1) : 704 + 64 * (z + 1), at], jnp.zeros((), BF))
            for z in range(8)
        ]
        moved = jnp.concatenate(
            [
                jnp.concatenate([pltpu.roll(o, shift % 128, 1) if shift else o for o in own], axis=1)
                for shift in SHIFTS
            ],
            axis=0,
        )
        total_ref[...] += lax.dot_general(
            moved, taps(planes_ref, slot, 0, 8), (((1,), (1,)), ((), ())), preferred_element_type=F32
        )
        return carry

    lax.fori_loop(0, 8, step, 0)
    scale = scale_ref[0]

    def part(k):
        if k == 27:
            return jnp.zeros((64, 64), F32)
        return total_ref[64 * (k % 9) : 64 * (k % 9) + 64, 64 * (k // 9) : 64 * (k // 9) + 64] * scale

    for j in range(14):
        terms_ref[64 * j : 64 * j + 64] = jnp.concatenate([part(2 * j), part(2 * j + 1)], axis=1)


def planes_and_terms(scale, place, x, g, below, above, pair, other):
    vmem = pl.BlockSpec(memory_space=pltpu.VMEM)
    return pl.pallas_call(
        terms_kernel,
        in_specs=[pl.BlockSpec(memory_space=pltpu.SMEM)] + [vmem] * 7,
        out_specs=[vmem, vmem],
        out_shape=[
            jax.ShapeDtypeStruct((1280, 1024), BF),
            jax.ShapeDtypeStruct((896, 128), F32),
        ],
        scratch_shapes=[pltpu.VMEM((1280, 768), BF), pltpu.VMEM((576, 192), F32)],
        compiler_params=params(),
        cost_estimate=pl.CostEstimate(flops=10**10, bytes_accessed=10**7, transcendentals=0),
        name="terms",
    )(scale, place, x, g, below, above, pair, other)


def conv_kernel(planes_ref, weight_ref, out_ref):
    row = iota((256, 128), 0)
    lane = row % 128
    y, x = lane // 10 - 1, lane % 10 - 1
    inner = (y >= 0) & (y < 8) & (x >= 0) & (x < 8)
    pick = jnp.where(
        inner & (iota((256, 128), 1) == (row // 128) * 64 + y * 8 + x), 1.0, 0.0
    ).astype(BF)

    def step(slot, carry):
        for zp in range(4):
            parts = jnp.dot(weight_ref[...], taps(planes_ref, slot, 2 * zp, 2), preferred_element_type=F32)
            tiles = []
            for h in range(2):
                total = None
                for m, shift in enumerate(SHIFTS):
                    piece = parts[64 * m : 64 * m + 64, 128 * h : 128 * h + 128]
                    if shift:
                        piece = pltpu.roll(piece, (-shift) % 128, 1)
                    total = piece if total is None else total + piece
                tiles.append(total.astype(BF))
            out_ref[slot, :, 128 * zp : 128 * zp + 128] = jnp.dot(
                jnp.concatenate(tiles, axis=1), pick, preferred_element_type=F32
            ).astype(BF)
        return carry

    lax.fori_loop(0, 8, step, 0)


def conv(planes, weight, which):
    return pl.pallas_call(
        conv_kernel,
        grid=(1,),
        in_specs=[
            pl.BlockSpec((640, 1024), lambda i: (which, 0)),
            pl.BlockSpec((576, 192), lambda i: (0, 0)),
        ],
        out_specs=pl.BlockSpec((8, 64, 512), lambda i: (0, 0, 0)),
        out_shape=jax.ShapeDtypeStruct((8, 64, 512), BF),
        compiler_params=params(),
        cost_estimate=pl.CostEstimate(flops=5 * 10**9, bytes_accessed=10**7, transcendentals=0),
        name="conv",
    )(planes, weight)


def coords(i):
    t = i % 64
    return [i // 64, t // 16, (t // 8) % 2, (t // 2) % 4, t % 2]


AXIS = {"zl": (0, 4), "y": (1, 4), "zh": (2, 2), "x": (3, 4), "c": (4, 2)}


def shift_pairs(key, by):
    at, size = AXIS[key]
    out = []
    for i in range(N_DEV):
        v = coords(i)
        v[at] = (v[at] + by) % size
        out.append((i, v[0] * 64 + ((v[1] * 2 + v[2]) * 4 + v[3]) * 2 + v[4]))
    return out


def send(x, key, by):
    return lax.ppermute(x, AXES, shift_pairs(key, by))


def scatter_sum(x, key, me):
    size = AXIS[key][1]
    parts = x.reshape(size, -1, x.shape[-1])
    total = lax.dynamic_index_in_dim(parts, me, 0, False)
    for s in range(1, size):
        total = total + send(lax.dynamic_index_in_dim(parts, (me + s) % size, 0, False), key, s)
    return total


def full_sum(x, key):
    total = x
    for s in range(1, AXIS[key][1]):
        total = total + send(x, key, s)
    return total


def gather(x, key, me):
    size = AXIS[key][1]
    found = jnp.stack([x] + [send(x, key, -s) for s in range(1, size)])
    return jnp.concatenate(
        [lax.dynamic_index_in_dim(found, (j - me) % size, 0, False) for j in range(size)], axis=0
    )


def total_over_devices(terms, slab, tile):
    core, x = tile % 2, (tile // 2) % 4
    part = scatter_sum(terms, "c", core)
    part = scatter_sum(part, "x", x)
    part = full_sum(part, "y")
    part = full_sum(part, "zl")
    part = full_sum(part, "zh")
    part = gather(part, "x", x)
    return gather(part, "c", core)


def shards(features, cotangent, weight, block_table):
    slab = lax.axis_index("slab")
    tile = lax.axis_index("tile")
    core = (tile % 2).astype(jnp.int32).reshape(1)
    table = jnp.pad(block_table, ((1, 1), (1, 1), (0, 0)), constant_values=-1)
    window = lax.dynamic_slice(table, (slab, tile * YR, 0), (3, 4, LX)).reshape(96)
    voxels = jnp.sum((block_table >= 0).astype(F32)) * 512.0
    scale = (1.0 / jnp.sqrt(voxels)).reshape(1)

    low, high = faces(features, cotangent)
    below = lax.ppermute(high, "slab", [(0, 1), (1, 2), (2, 3)])
    above = lax.ppermute(low, "slab", [(1, 0), (2, 1), (3, 2)])
    to_pair, to_other = edges(core, features, cotangent, below, above)
    pair = lax.ppermute(to_pair, "tile", [(i, i ^ 1) for i in range(64)])
    swaps = [(i, i + 1) for i in range(1, 63, 2)]
    other = lax.ppermute(to_other, "tile", swaps + [(b, a) for a, b in swaps])
    place = places(core, window)

    planes, terms = planes_and_terms(scale, place, features, cotangent, below, above, pair, other)
    spread = weight.reshape(64, 3, 9, 64)
    forward = spread.transpose(2, 0, 1, 3).reshape(576, 192)
    backward = spread[:, ::-1, ::-1].transpose(2, 3, 1, 0).reshape(576, 192)
    conv_out = conv(planes, forward, 0)
    grad_features = conv(planes, backward, 1)
    summed = total_over_devices(terms, slab, tile)
    grad_weight = summed.reshape(14, 64, 128).transpose(1, 0, 2).reshape(64, 1792)[:, :1728]
    return conv_out, grad_features, grad_weight


def solution(mesh):
    rows = P(AXES, None, None)
    return jax.shard_map(
        shards,
        mesh=mesh,
        in_specs=(rows, rows, P(), P()),
        out_specs=(rows, rows, P()),
        check_vma=False,
    )
```

```python
import functools

import jax
import jax.numpy as jnp
from jax import lax
from jax.experimental import pallas as pl
from jax.experimental.pallas import tpu as pltpu
from jax.sharding import PartitionSpec as P

LX = 8
YR = 2
BF = jnp.bfloat16
F32 = jnp.float32
AXES = ("slab", "tile")
N_DEV = 256
VMEM_LIMIT = 24 * 1024 * 1024
SHIFTS = [dy * 10 + dx for dy in (-1, 0, 1) for dx in (-1, 0, 1)]


def params():
    return pltpu.CompilerParams(vmem_limit_bytes=VMEM_LIMIT)


def iota(shape, dim):
    return lax.broadcasted_iota(jnp.int32, shape, dim)


def halves(a, b, right):
    cut = slice(64, 128) if right else slice(0, 64)
    return jnp.concatenate([a[:, cut], b[:, cut]], axis=1)


def in_hbm(x):
    return pltpu.with_memory_space_constraint(x, pltpu.HBM)


def in_vmem(x):
    return pltpu.with_memory_space_constraint(x, pltpu.VMEM)


def faces_kernel(x_ref, g_ref, low_ref, high_ref, xv_ref, gv_ref, sems):
    copies = [
        pltpu.make_async_copy(src.at[4 * h : 4 * h + 4], dst.at[4 * h : 4 * h + 4], sems.at[2 * h + i])
        for h in range(2)
        for i, (src, dst) in enumerate(((x_ref, xv_ref), (g_ref, gv_ref)))
    ]
    for copy in copies:
        copy.start()
    for h in range(2):
        for copy in copies[2 * h : 2 * h + 2]:
            copy.wait()
        for s in range(4 * h, 4 * h + 4):
            low_ref[s] = halves(xv_ref[s, :, :128], gv_ref[s, :, :128], False)
            high_ref[s] = halves(xv_ref[s, :, 384:], gv_ref[s, :, 384:], True)


def faces(x, g):
    vmem = pl.BlockSpec(memory_space=pltpu.VMEM)
    hbm = pl.BlockSpec(memory_space=pltpu.HBM)
    face = jax.ShapeDtypeStruct((8, 64, 128), BF)
    held = pltpu.VMEM((8, 64, 512), BF)
    return pl.pallas_call(
        faces_kernel,
        in_specs=[hbm, hbm],
        out_specs=[vmem] * 4,
        out_shape=[face, face, held, held],
        scratch_shapes=[pltpu.SemaphoreType.DMA((4,))],
        compiler_params=params(),
        name="faces",
    )(in_hbm(x), in_hbm(g))


def edges_kernel(core_ref, window_ref, scale_ref, x_ref, g_ref, below_ref, above_ref, pair_ref, other_ref):
    chunk = iota((1024, 128), 0) // 128
    lane = iota((1024, 128), 0) % 128
    to = iota((1024, 128), 1)

    def picks(y):
        here = (lane // 8) % 8 == y
        edge = (lane // 64) * 64 + chunk * 8 + lane % 8
        line = (chunk // 4) * 64 + (lane // 64) * 32 + (chunk % 4) * 8 + lane % 8
        return [
            jnp.where(here & (at == to), 1.0, 0.0).astype(BF) for at in (edge, line)
        ]

    found = []
    for first, y in ((4, 7), (0, 0)):
        edge, line = picks(y)
        rows = [
            jnp.concatenate(
                [ref[first + s, :, 128 * t : 128 * t + 128] for ref in (x_ref, g_ref) for s in range(4)],
                axis=1,
            )
            for t in range(4)
        ]
        lines = jnp.concatenate(
            [ref[first + s] for ref in (below_ref, above_ref) for s in range(4)], axis=1
        )
        main = jnp.dot(jnp.concatenate(rows, axis=0), edge, preferred_element_type=F32)
        last = jnp.dot(lines, line, preferred_element_type=F32)
        found.append(jnp.concatenate([main, last], axis=0))
    up, down = found
    odd = core_ref[0]
    pair_ref[...] = jnp.where(odd == 0, up, down).astype(BF)
    other_ref[...] = jnp.where(odd == 0, down, up).astype(BF)


def edges(core, window, scale, x, g, below, above):
    out = jax.ShapeDtypeStruct((320, 128), BF)
    vmem = pl.BlockSpec(memory_space=pltpu.VMEM)
    return pl.pallas_call(
        edges_kernel,
        in_specs=[pl.BlockSpec(memory_space=pltpu.SMEM)] * 3 + [vmem] * 4,
        out_specs=[vmem, vmem],
        out_shape=[out, out],
        compiler_params=params(),
        name="edges",
    )(core, window, scale, x, g, below, above)


def prepare_kernel(core_ref, table_ref, weight_hbm, place_ref, forward_ref, backward_ref, weight_ref, sem):
    load = pltpu.make_async_copy(weight_hbm, weight_ref, sem)
    load.start()
    fill_places(core_ref, table_ref, place_ref)
    load.wait()
    rows = iota((128, 128), 0)
    same = jnp.where(rows == iota((128, 128), 1), 1.0, 0.0).astype(BF)
    for k in range(27):
        dz, m = k // 9, k % 9
        forward_ref[64 * m : 64 * m + 64, 64 * dz : 64 * dz + 64] = weight_ref[:, 64 * k : 64 * k + 64]
    for j in range(14):
        wide = min(128, 1728 - 128 * j)
        turned = lax.dot_general(
            same[:wide, :wide],
            weight_ref[:, 128 * j : 128 * j + wide],
            (((1,), (1,)), ((), ())),
            preferred_element_type=F32,
        ).astype(BF)
        for k in range(2 * j, 2 * j + wide // 64):
            dz, m = (26 - k) // 9, (26 - k) % 9
            backward_ref[64 * m : 64 * m + 64, 64 * dz : 64 * dz + 64] = turned[64 * (k - 2 * j) : 64 * (k - 2 * j) + 64]


def fill_places(core_ref, table_ref, place_ref):
    odd = core_ref[0]
    lane = iota((8, 128), 1)
    ly = lane // 10 - 1
    lx = lane % 10 - 1
    used = lane < 100
    y_class = jnp.where(ly < 0, 0, jnp.where(ly > 7, 2, 1))
    x_class = jnp.where(lx < 0, 0, jnp.where(lx > 7, 2, 1))
    near = jnp.where(used, y_class * 3 + x_class, -1)
    inner_x = lx & 7
    inner = (ly & 7) * 8 + inner_x
    rows = iota((768, 128), 0)
    for s in range(8):
        r = s // 4
        column = jnp.int32(-10)
        for b in range(8):
            column = jnp.where(table_ref[(4 + r + 1) * 8 + b] == s, b, column)
        for d in range(3):
            source = jnp.full((8, 128), -1, jnp.int32)
            for dy in range(3):
                row = r + dy
                for dx in range(3):
                    at = column + (dx - 1)
                    inside = (at >= 0) & (at < LX)
                    held = table_ref[(d * 4 + row) * 8 + jnp.clip(at, 0, LX - 1)]
                    fine = inside & (held >= 0)
                    if row in (1, 2):
                        base = jnp.where(fine, held * 64, -10000)
                        value = base + inner
                    else:
                        side = 1 - odd if row == 0 else odd
                        base = jnp.where(fine, 512 + side * 128 + (held & 3) * 8, -10000)
                        value = base + inner_x
                    source = jnp.where(near == dy * 3 + dx, value, source)
            place_ref[d, :, 128 * s : 128 * s + 128] = jnp.where(
                rows == source[0:1], 1.0, 0.0
            ).astype(BF)


def prepare(core, window, weight):
    smem = pl.BlockSpec(memory_space=pltpu.SMEM)
    vmem = pl.BlockSpec(memory_space=pltpu.VMEM)
    turned = pltpu.VMEM((576, 192), BF)
    return pl.pallas_call(
        prepare_kernel,
        in_specs=[smem, smem, pl.BlockSpec(memory_space=pltpu.HBM)],
        out_specs=[vmem] * 3,
        out_shape=[pltpu.VMEM((3, 768, 1024), BF), turned, turned],
        scratch_shapes=[pltpu.VMEM((64, 1728), BF), pltpu.SemaphoreType.DMA],
        compiler_params=params(),
        name="prepare",
    )(core, window, in_hbm(weight))


def taps(planes_ref, slot, z_from, z_count):
    at = slice(128 * slot, 128 * slot + 128)
    return jnp.concatenate(
        [
            jnp.concatenate(
                [planes_ref[64 * (z + dz) : 64 * (z + dz) + 64, at] for z in range(z_from, z_from + z_count)],
                axis=1,
            )
            for dz in range(3)
        ],
        axis=0,
    )


def terms_kernel(core_ref, scale_ref, place_ref, x_ref, g_ref, below_ref, above_ref, pair_ref, other_ref, x_planes_ref, g_planes_ref, mine_ref, theirs_ref, left_ref, total_ref, even_ref, odd_ref):
    def fill(row, tiles, right, band, lane_group):
        for j in range(4):
            left_ref[row : row + 64, 128 * j : 128 * j + 128] = halves(tiles[2 * j], tiles[2 * j + 1], right)
        for side, ref in enumerate((pair_ref, other_ref)):
            tile = ref[64 * band : 64 * band + 64]
            if lane_group:
                tile = pltpu.roll(tile, 128 - 32 * lane_group, 1)
            left_ref[row : row + 64, 512 + 128 * side : 640 + 128 * side] = tile

    for a, ref in enumerate((x_ref, g_ref)):
        for t in range(4):
            tiles = [ref[s, :, 128 * t : 128 * t + 128] for s in range(8)]
            for parity in range(2):
                fill(512 * a + 64 * (2 * t + parity), tiles, parity, t, 2 * parity + a)
    for side, ref in enumerate((below_ref, above_ref)):
        tiles = [ref[s] for s in range(8)]
        for a in range(2):
            fill(1024 + 128 * side + 64 * a, tiles, a, 4, 2 * side + a)

    for a, ref in enumerate((x_planes_ref, g_planes_ref)):
        ref[64:576] = jnp.dot(
            left_ref[512 * a : 512 * a + 512], place_ref[1], preferred_element_type=F32
        ).astype(BF)
    for side in range(2):
        both = jnp.dot(
            left_ref[1024 + 128 * side : 1152 + 128 * side],
            place_ref[2 * side],
            preferred_element_type=F32,
        ).astype(BF)
        x_planes_ref[576 * side : 576 * side + 64] = both[:64]
        g_planes_ref[576 * side : 576 * side + 64] = both[64:]

    total_ref[...] = jnp.zeros_like(total_ref)
    lane = iota((64, 128), 1)
    column = lane % 10
    inner = (lane >= 10) & (lane < 90) & (column >= 1) & (column <= 8)

    def move(slot, moved_ref):
        for z in range(8):
            at = slice(128 * slot, 128 * slot + 128)
            own = jnp.where(inner, g_planes_ref[64 * (z + 1) : 64 * (z + 1) + 64, at], jnp.zeros((), BF))
            for m, shift in enumerate(SHIFTS):
                moved_ref[64 * m : 64 * m + 64, 128 * z : 128 * z + 128] = (
                    pltpu.roll(own, shift % 128, 1) if shift else own
                )

    move(0, even_ref)
    for slot in range(8):
        now, later = (even_ref, odd_ref) if slot % 2 == 0 else (odd_ref, even_ref)
        if slot < 7:
            move(slot + 1, later)
        total_ref[...] += lax.dot_general(
            now[...], taps(x_planes_ref, slot, 0, 8), (((1,), (1,)), ((), ())), preferred_element_type=F32
        )
    scale = scale_ref[0]

    def part(k):
        if k == 27:
            return jnp.zeros((64, 64), F32)
        return total_ref[64 * (k % 9) : 64 * (k % 9) + 64, 64 * (k // 9) : 64 * (k // 9) + 64] * scale

    def write(refs):
        for j in range(14):
            at = 64 * (j % 7)
            refs[j // 7][at : at + 64] = jnp.concatenate([part(2 * j), part(2 * j + 1)], axis=1)

    pl.when(core_ref[0] == 0)(lambda: write((mine_ref, theirs_ref)))
    pl.when(core_ref[0] == 1)(lambda: write((theirs_ref, mine_ref)))


def planes_and_terms(core, scale, place, x, g, below, above, pair, other):
    vmem = pl.BlockSpec(memory_space=pltpu.VMEM)
    return pl.pallas_call(
        terms_kernel,
        in_specs=[pl.BlockSpec(memory_space=pltpu.SMEM)] * 2 + [vmem] * 7,
        out_specs=[vmem] * 4,
        out_shape=[pltpu.VMEM((640, 1024), BF)] * 2 + [jax.ShapeDtypeStruct((448, 128), F32)] * 2,
        scratch_shapes=[pltpu.VMEM((1280, 768), BF), pltpu.VMEM((576, 192), F32)]
        + [pltpu.VMEM((576, 1024), BF)] * 2,
        compiler_params=params(),
        cost_estimate=pl.CostEstimate(flops=10**10, bytes_accessed=10**7, transcendentals=0),
        name="terms",
    )(core, scale, place, x, g, below, above, pair, other)


def conv_kernel(half, planes_ref, weight_ref, after_ref, *refs):
    out_hbm, token_ref, even_ref, odd_ref, out_ref, sems = refs[-6:]
    row = iota((256, 128), 0)
    lane = row % 128
    y, x = lane // 10 - 1, lane % 10 - 1
    inner = (y >= 0) & (y < 8) & (x >= 0) & (x < 8)
    pick = jnp.where(
        inner & (iota((256, 128), 1) == (row // 128) * 64 + y * 8 + x), 1.0, 0.0
    ).astype(BF)

    def store(slot):
        return pltpu.make_async_copy(out_ref.at[slot], out_hbm.at[4 * half + slot], sems.at[slot])

    def multiply(slot, parts_ref):
        for zp in range(4):
            parts_ref[:, 256 * zp : 256 * zp + 256] = jnp.dot(
                weight_ref[...], taps(planes_ref, 4 * half + slot, 2 * zp, 2), preferred_element_type=F32
            )

    def add(slot, parts_ref):
        for zp in range(4):
            tiles = []
            for h in range(2):
                at = 256 * zp + 128 * h
                total = None
                for m, shift in enumerate(SHIFTS):
                    piece = parts_ref[64 * m : 64 * m + 64, at : at + 128]
                    if shift:
                        piece = pltpu.roll(piece, (-shift) % 128, 1)
                    total = piece if total is None else total + piece
                tiles.append(total.astype(BF))
            out_ref[slot, :, 128 * zp : 128 * zp + 128] = jnp.dot(
                jnp.concatenate(tiles, axis=1), pick, preferred_element_type=F32
            ).astype(BF)

    multiply(0, even_ref)
    for slot in range(4):
        now, later = (even_ref, odd_ref) if slot % 2 == 0 else (odd_ref, even_ref)
        if slot < 3:
            multiply(slot + 1, later)
        add(slot, now)
        store(slot).start()
    for slot in range(4):
        store(slot).wait()
    token_ref[...] = jnp.zeros_like(token_ref)


def conv(planes, weight, half, after, into=None):
    anywhere = pl.BlockSpec(memory_space=pl.ANY)
    vmem = pl.BlockSpec(memory_space=pltpu.VMEM)
    hbm = pl.BlockSpec(memory_space=pltpu.HBM)
    return pl.pallas_call(
        functools.partial(conv_kernel, half),
        in_specs=[vmem, vmem, anywhere] + [hbm] * (into is not None),
        out_specs=[hbm, vmem],
        out_shape=[
            jax.ShapeDtypeStruct((8, 64, 512), BF),
            jax.ShapeDtypeStruct((8, 128), F32),
        ],
        scratch_shapes=[pltpu.VMEM((576, 1024), F32)] * 2
        + [pltpu.VMEM((4, 64, 512), BF), pltpu.SemaphoreType.DMA((4,))],
        input_output_aliases={} if into is None else {3: 0},
        compiler_params=params(),
        cost_estimate=pl.CostEstimate(flops=3 * 10**9, bytes_accessed=10**6, transcendentals=0),
        name="conv",
    )(in_vmem(planes), in_vmem(weight), after, *([] if into is None else [into]))


def coords(i):
    t = i % 64
    return [i // 64, t // 16, (t // 8) % 2, (t // 2) % 4, t % 2]


AXIS = {"zl": (0, 4), "y": (1, 4), "zh": (2, 2), "x": (3, 4), "c": (4, 2)}


def shift_pairs(key, by):
    at, size = AXIS[key]
    out = []
    for i in range(N_DEV):
        v = coords(i)
        v[at] = (v[at] + by) % size
        out.append((i, v[0] * 64 + ((v[1] * 2 + v[2]) * 4 + v[3]) * 2 + v[4]))
    return out


def send(x, key, by):
    return lax.ppermute(x, AXES, shift_pairs(key, by))


def plus(terms, token=None):
    vmem = pl.BlockSpec(memory_space=pltpu.VMEM)
    tokens = [] if token is None else [token]

    def kernel(*refs):
        *parts, out_ref = refs[len(tokens) :]
        out_ref[...] = functools.reduce(jnp.add, [ref[...] for ref in parts])

    return pl.pallas_call(
        kernel,
        in_specs=[pl.BlockSpec(memory_space=pl.ANY)] * len(tokens) + [vmem] * len(terms),
        out_specs=vmem,
        out_shape=jax.ShapeDtypeStruct(terms[0].shape, F32),
        compiler_params=params(),
        name="plus",
    )(*tokens, *terms)


def cut_kernel(me_ref, mine_ref, got_ref, *refs):
    *out_refs, total_ref = refs
    total_ref[...] = mine_ref[...] + got_ref[...]
    for s, ref in enumerate(out_refs):
        at = lax.rem(me_ref[0] + s, 4) * 112
        ref[...] = total_ref[pl.ds(pl.multiple_of(at, 8), 112)]


def cut(me, mine, got):
    vmem = pl.BlockSpec(memory_space=pltpu.VMEM)
    return pl.pallas_call(
        cut_kernel,
        in_specs=[pl.BlockSpec(memory_space=pltpu.SMEM), vmem, vmem],
        out_specs=[vmem] * 4,
        out_shape=[jax.ShapeDtypeStruct((112, 128), F32)] * 4,
        scratch_shapes=[pltpu.VMEM((448, 128), F32)],
        compiler_params=params(),
        name="cut",
    )(me, mine, got)


def assemble_kernel(me_ref, token_ref, *refs):
    *parts, out_ref = refs
    rows = parts[0].shape[0]
    for s, ref in enumerate(parts):
        at = lax.rem(me_ref[0] + s, len(parts)) * rows
        out_ref[pl.ds(pl.multiple_of(at, 8), rows)] = ref[...]


def assemble(me, parts, token):
    vmem = pl.BlockSpec(memory_space=pltpu.VMEM)
    rows = parts[0].shape[0]
    return pl.pallas_call(
        assemble_kernel,
        in_specs=[pl.BlockSpec(memory_space=pltpu.SMEM), pl.BlockSpec(memory_space=pl.ANY)] + [vmem] * len(parts),
        out_specs=vmem,
        out_shape=jax.ShapeDtypeStruct((rows * len(parts), 128), F32),
        compiler_params=params(),
        name="assemble",
    )(me, token, *parts)


def finish_kernel(me_ref, mine_ref, other_ref, out_ref):
    def fill(parts):
        for j in range(14):
            wide = 64 if j == 13 else 128
            out_ref[:, 128 * j : 128 * j + wide] = parts[j // 7][64 * (j % 7) : 64 * (j % 7) + 64, :wide]

    pl.when(me_ref[0] == 0)(lambda: fill((mine_ref, other_ref)))
    pl.when(me_ref[0] == 1)(lambda: fill((other_ref, mine_ref)))


def finish(me, mine, other):
    vmem = pl.BlockSpec(memory_space=pltpu.VMEM)
    return pl.pallas_call(
        finish_kernel,
        in_specs=[pl.BlockSpec(memory_space=pltpu.SMEM), vmem, vmem],
        out_specs=vmem,
        out_shape=jax.ShapeDtypeStruct((64, 1728), F32),
        compiler_params=params(),
        name="finish",
    )(me, mine, other)


def shards(features, cotangent, weight, block_table):
    slab = lax.axis_index("slab")
    tile = lax.axis_index("tile")
    core = (tile % 2).astype(jnp.int32).reshape(1)
    table = jnp.pad(block_table, ((1, 1), (1, 1), (0, 0)), constant_values=-1)
    window = lax.dynamic_slice(table, (slab, tile * YR, 0), (3, 4, LX)).reshape(96)
    voxels = jnp.sum((block_table >= 0).astype(F32)) * 512.0
    scale = (1.0 / jnp.sqrt(voxels)).reshape(1)

    low, high, x_held, g_held = faces(features, cotangent)
    below = lax.ppermute(high, "slab", [(0, 1), (1, 2), (2, 3)])
    above = lax.ppermute(low, "slab", [(1, 0), (2, 1), (3, 2)])
    to_pair, to_other = edges(core, window, scale, x_held, g_held, below, above)
    pair = lax.ppermute(to_pair, "tile", [(i, i ^ 1) for i in range(64)])
    swaps = [(i, i + 1) for i in range(1, 63, 2)]
    other = lax.ppermute(to_other, "tile", swaps + [(b, a) for a, b in swaps])
    place, forward, backward = prepare(core, window, weight)

    x_planes, g_planes, mine, theirs = planes_and_terms(core, scale, place, x_held, g_held, below, above, pair, other)

    x = ((tile // 2) % 4).astype(jnp.int32).reshape(1)
    quarters = cut(x, mine, send(theirs, "c", 1))
    part = quarters[0]

    got = [send(quarters[s], "x", s) for s in (2, 3, 1)]
    conv_out, token = conv(x_planes, forward, 0, part)
    part = plus([part] + got, token)

    got = [send(part, "y", s) for s in (2, 3, 1)]
    conv_out, token = conv(x_planes, forward, 1, part, conv_out)
    part = plus([part] + got, token)

    got = [send(part, "zl", s) for s in (2, 3, 1)]
    grad_features, token = conv(g_planes, backward, 0, part)
    part = plus([part] + got, token)

    part = plus([part, send(part, "zh", 1)])

    got = [send(part, "x", -s) for s in (1, 2, 3)]
    grad_features, token = conv(g_planes, backward, 1, part, grad_features)
    half = assemble(x, [part] + got, token)

    grad_weight = finish(core, half, send(half, "c", 1))
    return conv_out, grad_features, grad_weight


def solution(mesh):
    rows = P(AXES, None, None)
    return jax.shard_map(
        shards,
        mesh=mesh,
        in_specs=(rows, rows, P(), P()),
        out_specs=(rows, rows, P()),
        check_vma=False,
    )
```

```python
import functools

import jax
import jax.numpy as jnp
from jax import lax
from jax.experimental import pallas as pl
from jax.experimental.pallas import tpu as pltpu
from jax.sharding import PartitionSpec as P

LX = 8
YR = 2
BF = jnp.bfloat16
F32 = jnp.float32
AXES = ("slab", "tile")
N_DEV = 256
MIB = 1024 * 1024
SHIFTS = [dy * 10 + dx for dy in (-1, 0, 1) for dx in (-1, 0, 1)]


def params(mib=6):
    return pltpu.CompilerParams(vmem_limit_bytes=mib * MIB)


def iota(shape, dim):
    return lax.broadcasted_iota(jnp.int32, shape, dim)


def halves(a, b, right):
    cut = slice(64, 128) if right else slice(0, 64)
    return jnp.concatenate([a[:, cut], b[:, cut]], axis=1)


def in_hbm(x):
    return pltpu.with_memory_space_constraint(x, pltpu.HBM)


def in_vmem(x):
    return pltpu.with_memory_space_constraint(x, pltpu.VMEM)


def edges_kernel(core_ref, x_ref, g_ref, pair_ref, other_ref, xv_ref, gv_ref, sems):
    copies = [
        pltpu.make_async_copy(src.at[4 * h : 4 * h + 4], dst.at[4 * h : 4 * h + 4], sems.at[2 * h + i])
        for h in range(2)
        for i, (src, dst) in enumerate(((x_ref, xv_ref), (g_ref, gv_ref)))
    ]
    for copy in copies:
        copy.start()
    chunk = iota((1024, 128), 0) // 128
    lane = iota((1024, 128), 0) % 128
    at = (lane // 64) * 64 + chunk * 8 + lane % 8
    match = at == iota((1024, 128), 1)
    found = []
    for h, y in ((0, 0), (1, 7)):
        edge = jnp.where(match & ((lane // 8) % 8 == y), 1.0, 0.0).astype(BF)
        for copy in copies[2 * h : 2 * h + 2]:
            copy.wait()
        rows = [
            jnp.concatenate(
                [ref[4 * h + s, :, 128 * t : 128 * t + 128] for ref in (xv_ref, gv_ref) for s in range(4)],
                axis=1,
            )
            for t in range(4)
        ]
        found.append(jnp.dot(jnp.concatenate(rows, axis=0), edge, preferred_element_type=F32))
    down, up = found
    odd = core_ref[0]
    pair_ref[...] = jnp.where(odd == 0, up, down).astype(BF)
    other_ref[...] = jnp.where(odd == 0, down, up).astype(BF)


def edges(core, x, g):
    vmem = pl.BlockSpec(memory_space=pltpu.VMEM)
    hbm = pl.BlockSpec(memory_space=pltpu.HBM)
    edge = jax.ShapeDtypeStruct((256, 128), BF)
    held = pltpu.VMEM((8, 64, 512), BF)
    return pl.pallas_call(
        edges_kernel,
        in_specs=[pl.BlockSpec(memory_space=pltpu.SMEM), hbm, hbm],
        out_specs=[vmem] * 4,
        out_shape=[edge, edge, held, held],
        scratch_shapes=[pltpu.SemaphoreType.DMA((4,))],
        compiler_params=params(12),
        name="edges",
    )(core, in_hbm(x), in_hbm(g))


def faces_kernel(x_ref, g_ref, low_ref, high_ref):
    for s in range(8):
        low_ref[s] = halves(x_ref[s, :, :128], g_ref[s, :, :128], False)
        high_ref[s] = halves(x_ref[s, :, 384:], g_ref[s, :, 384:], True)


def faces(x, g):
    vmem = pl.BlockSpec(memory_space=pltpu.VMEM)
    return pl.pallas_call(
        faces_kernel,
        in_specs=[vmem, vmem],
        out_specs=[vmem, vmem],
        out_shape=[jax.ShapeDtypeStruct((8, 64, 128), BF)] * 2,
        compiler_params=params(8),
        name="faces",
    )(in_vmem(x), in_vmem(g))


def lines_kernel(pair_ref, other_ref, low_ref, high_ref):
    low_ref[...] = halves(pair_ref[:64], other_ref[:64], False)
    high_ref[...] = halves(pair_ref[192:], other_ref[192:], True)


def lines(pair, other):
    vmem = pl.BlockSpec(memory_space=pltpu.VMEM)
    return pl.pallas_call(
        lines_kernel,
        in_specs=[vmem, vmem],
        out_specs=[vmem, vmem],
        out_shape=[jax.ShapeDtypeStruct((64, 128), BF)] * 2,
        compiler_params=params(),
        name="lines",
    )(pair, other)


def weights_kernel(after_ref, blocks_ref, weight_hbm, forward_ref, backward_ref, scale_ref, weight_ref, sem):
    load = pltpu.make_async_copy(weight_hbm, weight_ref, sem)
    load.start()
    active = jnp.sum(jnp.where(blocks_ref[...] >= 0, 1.0, 0.0), axis=0)
    voxels = jnp.sum(jnp.sum(active, axis=1, keepdims=True), axis=0, keepdims=True) * 512.0
    scale_ref[...] = jnp.broadcast_to(1.0 / jnp.sqrt(voxels), (8, 128))
    load.wait()
    rows = iota((128, 128), 0)
    same = jnp.where(rows == iota((128, 128), 1), 1.0, 0.0).astype(BF)
    for k in range(27):
        dz, m = k // 9, k % 9
        forward_ref[64 * m : 64 * m + 64, 64 * dz : 64 * dz + 64] = weight_ref[:, 64 * k : 64 * k + 64]
    for j in range(14):
        wide = min(128, 1728 - 128 * j)
        turned = lax.dot_general(
            same[:wide, :wide],
            weight_ref[:, 128 * j : 128 * j + wide],
            (((1,), (1,)), ((), ())),
            preferred_element_type=F32,
        ).astype(BF)
        for k in range(2 * j, 2 * j + wide // 64):
            dz, m = (26 - k) // 9, (26 - k) % 9
            backward_ref[64 * m : 64 * m + 64, 64 * dz : 64 * dz + 64] = turned[64 * (k - 2 * j) : 64 * (k - 2 * j) + 64]


def arranged_weights(weight, blocks, after):
    vmem = pl.BlockSpec(memory_space=pltpu.VMEM)
    turned = pltpu.VMEM((576, 192), BF)
    return pl.pallas_call(
        weights_kernel,
        in_specs=[pl.BlockSpec(memory_space=pl.ANY), vmem, pl.BlockSpec(memory_space=pltpu.HBM)],
        out_specs=[vmem] * 3,
        out_shape=[turned, turned, jax.ShapeDtypeStruct((8, 128), F32)],
        scratch_shapes=[pltpu.VMEM((64, 1728), BF), pltpu.SemaphoreType.DMA],
        compiler_params=params(),
        name="weights",
    )(after, blocks, in_hbm(weight))


def fill_places(core_ref, table_ref, place_ref):
    odd = core_ref[0]
    lane = iota((8, 128), 1)
    ly = lane // 10 - 1
    lx = lane % 10 - 1
    used = lane < 100
    y_class = jnp.where(ly < 0, 0, jnp.where(ly > 7, 2, 1))
    x_class = jnp.where(lx < 0, 0, jnp.where(lx > 7, 2, 1))
    near = jnp.where(used, y_class * 3 + x_class, -1)
    inner_x = lx & 7
    inner = (ly & 7) * 8 + inner_x
    rows = iota((768, 128), 0)
    for s in range(8):
        r = s // 4
        column = jnp.int32(-10)
        for b in range(8):
            column = jnp.where(table_ref[(4 + r + 1) * 8 + b] == s, b, column)
        for d in range(3):
            source = jnp.full((8, 128), -1, jnp.int32)
            for dy in range(3):
                row = r + dy
                for dx in range(3):
                    at = column + (dx - 1)
                    inside = (at >= 0) & (at < LX)
                    held = table_ref[(d * 4 + row) * 8 + jnp.clip(at, 0, LX - 1)]
                    fine = inside & (held >= 0)
                    if row in (1, 2):
                        base = jnp.where(fine, held * 64, -10000)
                        value = base + inner
                    else:
                        side = 1 - odd if row == 0 else odd
                        base = jnp.where(fine, 512 + side * 128 + (held & 3) * 8, -10000)
                        value = base + inner_x
                    source = jnp.where(near == dy * 3 + dx, value, source)
            place_ref[d, :, 128 * s : 128 * s + 128] = jnp.where(
                rows == source[0:1], 1.0, 0.0
            ).astype(BF)


def places(core, window):
    smem = pl.BlockSpec(memory_space=pltpu.SMEM)
    return pl.pallas_call(
        fill_places,
        in_specs=[smem, smem],
        out_specs=pl.BlockSpec(memory_space=pltpu.VMEM),
        out_shape=pltpu.VMEM((3, 768, 1024), BF),
        compiler_params=params(12),
        name="places",
    )(core, window)


def taps(planes_ref, z_from, z_count):
    return jnp.concatenate(
        [
            jnp.concatenate(
                [planes_ref[64 * (z + dz) : 64 * (z + dz) + 64] for z in range(z_from, z_from + z_count)],
                axis=1,
            )
            for dz in range(3)
        ],
        axis=0,
    )


def terms_kernel(core_ref, place_ref, x_ref, g_ref, below_ref, above_ref, below_line_ref, above_line_ref, pair_ref, other_ref, xa_ref, xb_hbm, ga_hbm, gb_hbm, mine_ref, theirs_ref, left_ref, total_ref, even_ref, odd_ref, xb_ref, ga_ref, gb_ref, sems):
    def fill(row, tiles, right, sides):
        for j in range(4):
            left_ref[row : row + 64, 128 * j : 128 * j + 128] = halves(tiles[2 * j], tiles[2 * j + 1], right)
        for side, (tile, lane_group) in enumerate(sides):
            if lane_group:
                tile = pltpu.roll(tile, 128 - 32 * lane_group, 1)
            left_ref[row : row + 64, 512 + 128 * side : 640 + 128 * side] = tile

    for a, ref in enumerate((x_ref, g_ref)):
        for t in range(4):
            tiles = [ref[s, :, 128 * t : 128 * t + 128] for s in range(8)]
            band = [edge[64 * t : 64 * t + 64] for edge in (pair_ref, other_ref)]
            for parity in range(2):
                fill(512 * a + 64 * (2 * t + parity), tiles, parity, [(tile, 2 * parity + a) for tile in band])
    for side, (ref, line_ref) in enumerate(((below_ref, below_line_ref), (above_ref, above_line_ref))):
        tiles = [ref[s] for s in range(8)]
        line = line_ref[...]
        for a in range(2):
            fill(1024 + 128 * side + 64 * a, tiles, a, [(line, a), (line, 2 + a)])

    x_planes = [(xa_ref, xb_ref)[slot // 4].at[slot % 4] for slot in range(8)]
    g_planes = [(ga_ref, gb_ref)[slot // 4].at[slot % 4] for slot in range(8)]
    for a, planes in enumerate((x_planes, g_planes)):
        main = jnp.dot(
            left_ref[512 * a : 512 * a + 512], place_ref[1], preferred_element_type=F32
        ).astype(BF)
        for slot in range(8):
            planes[slot][64:576] = main[:, 128 * slot : 128 * slot + 128]
    for side in range(2):
        both = jnp.dot(
            left_ref[1024 + 128 * side : 1152 + 128 * side],
            place_ref[2 * side],
            preferred_element_type=F32,
        ).astype(BF)
        for slot in range(8):
            at = slice(128 * slot, 128 * slot + 128)
            x_planes[slot][576 * side : 576 * side + 64] = both[:64, at]
            g_planes[slot][576 * side : 576 * side + 64] = both[64:, at]

    stores = [
        pltpu.make_async_copy(src, dst, sems.at[i])
        for i, (src, dst) in enumerate(((xb_ref, xb_hbm), (ga_ref, ga_hbm), (gb_ref, gb_hbm)))
    ]
    for store in stores:
        store.start()
    total_ref[...] = jnp.zeros_like(total_ref)
    lane = iota((64, 128), 1)
    column = lane % 10
    inner = (lane >= 10) & (lane < 90) & (column >= 1) & (column <= 8)

    def move(slot, moved_ref):
        for z in range(8):
            own = jnp.where(inner, g_planes[slot][64 * (z + 1) : 64 * (z + 1) + 64], jnp.zeros((), BF))
            for m, shift in enumerate(SHIFTS):
                moved_ref[64 * m : 64 * m + 64, 128 * z : 128 * z + 128] = (
                    pltpu.roll(own, shift % 128, 1) if shift else own
                )

    move(0, even_ref)
    for slot in range(8):
        now, later = (even_ref, odd_ref) if slot % 2 == 0 else (odd_ref, even_ref)
        if slot < 7:
            move(slot + 1, later)
        total_ref[...] += lax.dot_general(
            now[...], taps(x_planes[slot], 0, 8), (((1,), (1,)), ((), ())), preferred_element_type=F32
        )

    def part(k):
        if k == 27:
            return jnp.zeros((64, 64), F32)
        return total_ref[64 * (k % 9) : 64 * (k % 9) + 64, 64 * (k // 9) : 64 * (k // 9) + 64]

    def write(refs):
        for j in range(14):
            at = 64 * (j % 7)
            refs[j // 7][at : at + 64] = jnp.concatenate([part(2 * j), part(2 * j + 1)], axis=1)

    pl.when(core_ref[0] == 0)(lambda: write((mine_ref, theirs_ref)))
    pl.when(core_ref[0] == 1)(lambda: write((theirs_ref, mine_ref)))
    for store in stores:
        store.wait()


def planes_and_terms(core, place, x, g, *halo):
    vmem = pl.BlockSpec(memory_space=pltpu.VMEM)
    return pl.pallas_call(
        terms_kernel,
        in_specs=[pl.BlockSpec(memory_space=pltpu.SMEM)] + [vmem] * 9,
        out_specs=[vmem] + [pl.BlockSpec(memory_space=pltpu.HBM)] * 3 + [vmem] * 2,
        out_shape=[pltpu.VMEM((4, 640, 128), BF)] + [pltpu.HBM((4, 640, 128), BF)] * 3 + [jax.ShapeDtypeStruct((448, 128), F32)] * 2,
        scratch_shapes=[pltpu.VMEM((1280, 768), BF), pltpu.VMEM((576, 192), F32)]
        + [pltpu.VMEM((576, 1024), BF)] * 2
        + [pltpu.VMEM((4, 640, 128), BF)] * 3
        + [pltpu.SemaphoreType.DMA((3,))],
        compiler_params=params(24),
        cost_estimate=pl.CostEstimate(flops=10**10, bytes_accessed=10**7, transcendentals=0),
        name="terms",
    )(core, place, x, g, *halo)


def conv_kernel(half, planes_ref, weight_ref, after_ref, *refs):
    out_hbm, token_ref, even_ref, odd_ref, out_ref, sems = refs[-6:]
    row = iota((256, 128), 0)
    lane = row % 128
    y, x = lane // 10 - 1, lane % 10 - 1
    inner = (y >= 0) & (y < 8) & (x >= 0) & (x < 8)
    pick = jnp.where(
        inner & (iota((256, 128), 1) == (row // 128) * 64 + y * 8 + x), 1.0, 0.0
    ).astype(BF)

    def store(slot):
        return pltpu.make_async_copy(out_ref.at[slot], out_hbm.at[4 * half + slot], sems.at[slot])

    def multiply(slot, parts_ref):
        for zp in range(4):
            parts_ref[:, 256 * zp : 256 * zp + 256] = jnp.dot(
                weight_ref[...], taps(planes_ref.at[slot], 2 * zp, 2), preferred_element_type=F32
            )

    def add(slot, parts_ref):
        for zp in range(4):
            tiles = []
            for h in range(2):
                at = 256 * zp + 128 * h
                total = None
                for m, shift in enumerate(SHIFTS):
                    piece = parts_ref[64 * m : 64 * m + 64, at : at + 128]
                    if shift:
                        piece = pltpu.roll(piece, (-shift) % 128, 1)
                    total = piece if total is None else total + piece
                tiles.append(total.astype(BF))
            out_ref[slot, :, 128 * zp : 128 * zp + 128] = jnp.dot(
                jnp.concatenate(tiles, axis=1), pick, preferred_element_type=F32
            ).astype(BF)

    multiply(0, even_ref)
    for slot in range(4):
        now, later = (even_ref, odd_ref) if slot % 2 == 0 else (odd_ref, even_ref)
        if slot < 3:
            multiply(slot + 1, later)
        add(slot, now)
        store(slot).start()
    for slot in range(4):
        store(slot).wait()
    token_ref[...] = jnp.zeros_like(token_ref)


def conv(planes, weight, half, after, into=None):
    anywhere = pl.BlockSpec(memory_space=pl.ANY)
    vmem = pl.BlockSpec(memory_space=pltpu.VMEM)
    hbm = pl.BlockSpec(memory_space=pltpu.HBM)
    return pl.pallas_call(
        functools.partial(conv_kernel, half),
        in_specs=[vmem, vmem, anywhere] + [hbm] * (into is not None),
        out_specs=[hbm, vmem],
        out_shape=[
            jax.ShapeDtypeStruct((8, 64, 512), BF),
            jax.ShapeDtypeStruct((8, 128), F32),
        ],
        scratch_shapes=[pltpu.VMEM((576, 1024), F32)] * 2
        + [pltpu.VMEM((4, 64, 512), BF), pltpu.SemaphoreType.DMA((4,))],
        input_output_aliases={} if into is None else {3: 0},
        compiler_params=params(16),
        cost_estimate=pl.CostEstimate(flops=3 * 10**9, bytes_accessed=10**6, transcendentals=0),
        name="conv",
    )(in_vmem(planes), in_vmem(weight), after, *([] if into is None else [into]))


def coords(i):
    t = i % 64
    return [i // 64, t // 16, (t // 8) % 2, (t // 2) % 4, t % 2]


AXIS = {"zl": (0, 4), "y": (1, 4), "zh": (2, 2), "x": (3, 4), "c": (4, 2)}


def shift_pairs(key, by):
    at, size = AXIS[key]
    out = []
    for i in range(N_DEV):
        v = coords(i)
        v[at] = (v[at] + by) % size
        out.append((i, v[0] * 64 + ((v[1] * 2 + v[2]) * 4 + v[3]) * 2 + v[4]))
    return out


def send(x, key, by):
    return lax.ppermute(x, AXES, shift_pairs(key, by))


def plus(terms, token=None):
    vmem = pl.BlockSpec(memory_space=pltpu.VMEM)
    tokens = [] if token is None else [token]

    def kernel(*refs):
        *parts, out_ref = refs[len(tokens) :]
        out_ref[...] = functools.reduce(jnp.add, [ref[...] for ref in parts])

    return pl.pallas_call(
        kernel,
        in_specs=[pl.BlockSpec(memory_space=pl.ANY)] * len(tokens) + [vmem] * len(terms),
        out_specs=vmem,
        out_shape=jax.ShapeDtypeStruct(terms[0].shape, F32),
        compiler_params=params(),
        name="plus",
    )(*tokens, *terms)


def cut_kernel(me_ref, mine_ref, got_ref, *refs):
    *out_refs, total_ref = refs
    total_ref[...] = mine_ref[...] + got_ref[...]
    for s, ref in enumerate(out_refs):
        at = lax.rem(me_ref[0] + s, 4) * 112
        ref[...] = total_ref[pl.ds(pl.multiple_of(at, 8), 112)]


def cut(me, mine, got):
    vmem = pl.BlockSpec(memory_space=pltpu.VMEM)
    return pl.pallas_call(
        cut_kernel,
        in_specs=[pl.BlockSpec(memory_space=pltpu.SMEM), vmem, vmem],
        out_specs=[vmem] * 4,
        out_shape=[jax.ShapeDtypeStruct((112, 128), F32)] * 4,
        scratch_shapes=[pltpu.VMEM((448, 128), F32)],
        compiler_params=params(),
        name="cut",
    )(me, mine, got)


def assemble_kernel(me_ref, token_ref, *refs):
    *parts, out_ref = refs
    rows = parts[0].shape[0]
    for s, ref in enumerate(parts):
        at = lax.rem(me_ref[0] + s, len(parts)) * rows
        out_ref[pl.ds(pl.multiple_of(at, 8), rows)] = ref[...]


def assemble(me, parts, token):
    vmem = pl.BlockSpec(memory_space=pltpu.VMEM)
    rows = parts[0].shape[0]
    return pl.pallas_call(
        assemble_kernel,
        in_specs=[pl.BlockSpec(memory_space=pltpu.SMEM), pl.BlockSpec(memory_space=pl.ANY)] + [vmem] * len(parts),
        out_specs=vmem,
        out_shape=jax.ShapeDtypeStruct((rows * len(parts), 128), F32),
        compiler_params=params(),
        name="assemble",
    )(me, token, *parts)


def finish_kernel(me_ref, scale_ref, mine_ref, other_ref, out_ref):
    def fill(parts):
        for j in range(14):
            wide = 64 if j == 13 else 128
            out_ref[:, 128 * j : 128 * j + wide] = (
                parts[j // 7][64 * (j % 7) : 64 * (j % 7) + 64, :wide] * scale_ref[0:1, :wide]
            )

    pl.when(me_ref[0] == 0)(lambda: fill((mine_ref, other_ref)))
    pl.when(me_ref[0] == 1)(lambda: fill((other_ref, mine_ref)))


def finish(me, scale, mine, other):
    vmem = pl.BlockSpec(memory_space=pltpu.VMEM)
    return pl.pallas_call(
        finish_kernel,
        in_specs=[pl.BlockSpec(memory_space=pltpu.SMEM)] + [vmem] * 3,
        out_specs=vmem,
        out_shape=jax.ShapeDtypeStruct((64, 1728), F32),
        compiler_params=params(),
        name="finish",
    )(me, scale, mine, other)


def shards(features, cotangent, weight, block_table):
    slab = lax.axis_index("slab")
    tile = lax.axis_index("tile")
    core = (tile % 2).astype(jnp.int32).reshape(1)
    table = jnp.pad(block_table, ((1, 1), (1, 1), (0, 0)), constant_values=-1)
    window = lax.dynamic_slice(table, (slab, tile * YR, 0), (3, 4, LX)).reshape(96)
    to_pair, to_other, x_held, g_held = edges(core, features, cotangent)
    swaps = [(i, i + 1) for i in range(1, 63, 2)]
    other = lax.ppermute(to_other, "tile", swaps + [(b, a) for a, b in swaps])
    pair = lax.ppermute(to_pair, "tile", [(i, i ^ 1) for i in range(64)])
    rise, fall = [(0, 1), (1, 2), (2, 3)], [(1, 0), (2, 1), (3, 2)]
    low, high = faces(x_held, g_held)
    below = lax.ppermute(high, "slab", rise)
    above = lax.ppermute(low, "slab", fall)
    low_line, high_line = lines(pair, other)
    below_line = lax.ppermute(high_line, "slab", rise)
    above_line = lax.ppermute(low_line, "slab", fall)
    place = places(core, window)

    xa, xb, ga, gb, mine, theirs = planes_and_terms(
        core, place, x_held, g_held, below, above, below_line, above_line, pair, other
    )

    x = ((tile // 2) % 4).astype(jnp.int32).reshape(1)
    quarters = cut(x, mine, send(theirs, "c", 1))
    part = quarters[0]

    got = [send(quarters[s], "x", s) for s in (2, 3, 1)]
    forward, backward, scale = arranged_weights(weight, block_table, part)
    part = plus([part] + got, scale)

    got = [send(part, "y", s) for s in (2, 3, 1)]
    conv_out, token = conv(xa, forward, 0, part)
    part = plus([part] + got, token)

    got = [send(part, "zl", s) for s in (2, 3, 1)]
    conv_out, token = conv(xb, forward, 1, part, conv_out)
    part = plus([part] + got, token)

    got = send(part, "zh", 1)
    grad_features, token = conv(ga, backward, 0, part)
    part = plus([part, got], token)

    got = [send(part, "x", -s) for s in (1, 2, 3)]
    grad_features, token = conv(gb, backward, 1, part, grad_features)
    half = assemble(x, [part] + got, token)

    grad_weight = finish(core, scale, half, send(half, "c", 1))
    return conv_out, grad_features, grad_weight


def solution(mesh):
    rows = P(AXES, None, None)
    return jax.shard_map(
        shards,
        mesh=mesh,
        in_specs=(rows, rows, P(), P()),
        out_specs=(rows, rows, P()),
        check_vma=False,
    )
```

```python
import functools

import jax
import jax.numpy as jnp
from jax import lax
from jax.experimental import pallas as pl
from jax.experimental.pallas import tpu as pltpu
from jax.sharding import PartitionSpec as P

LX = 8
YR = 2
BF = jnp.bfloat16
F32 = jnp.float32
AXES = ("slab", "tile")
N_DEV = 256
MIB = 1024 * 1024
SHIFTS = [dy * 10 + dx for dy in (-1, 0, 1) for dx in (-1, 0, 1)]


def params(mib=6):
    return pltpu.CompilerParams(vmem_limit_bytes=mib * MIB)


def iota(shape, dim):
    return lax.broadcasted_iota(jnp.int32, shape, dim)


def halves(a, b, right):
    cut = slice(64, 128) if right else slice(0, 64)
    return jnp.concatenate([a[:, cut], b[:, cut]], axis=1)


def in_hbm(x):
    return pltpu.with_memory_space_constraint(x, pltpu.HBM)


def in_vmem(x):
    return pltpu.with_memory_space_constraint(x, pltpu.VMEM)


def edges_kernel(core_ref, x_ref, g_ref, pair_ref, other_ref, xv_ref, gv_ref, sems):
    copies = [
        pltpu.make_async_copy(src.at[4 * h : 4 * h + 4], dst.at[4 * h : 4 * h + 4], sems.at[2 * h + i])
        for h in range(2)
        for i, (src, dst) in enumerate(((x_ref, xv_ref), (g_ref, gv_ref)))
    ]
    for copy in copies:
        copy.start()
    chunk = iota((1024, 128), 0) // 128
    lane = iota((1024, 128), 0) % 128
    at = (lane // 64) * 64 + chunk * 8 + lane % 8
    match = at == iota((1024, 128), 1)
    found = []
    for h, y in ((0, 0), (1, 7)):
        edge = jnp.where(match & ((lane // 8) % 8 == y), 1.0, 0.0).astype(BF)
        for copy in copies[2 * h : 2 * h + 2]:
            copy.wait()
        rows = [
            jnp.concatenate(
                [ref[4 * h + s, :, 128 * t : 128 * t + 128] for ref in (xv_ref, gv_ref) for s in range(4)],
                axis=1,
            )
            for t in range(4)
        ]
        found.append(jnp.dot(jnp.concatenate(rows, axis=0), edge, preferred_element_type=F32))
    down, up = found
    odd = core_ref[0]
    pair_ref[...] = jnp.where(odd == 0, up, down).astype(BF)
    other_ref[...] = jnp.where(odd == 0, down, up).astype(BF)


def edges(core, x, g):
    vmem = pl.BlockSpec(memory_space=pltpu.VMEM)
    hbm = pl.BlockSpec(memory_space=pltpu.HBM)
    edge = jax.ShapeDtypeStruct((256, 128), BF)
    held = pltpu.VMEM((8, 64, 512), BF)
    return pl.pallas_call(
        edges_kernel,
        in_specs=[pl.BlockSpec(memory_space=pltpu.SMEM), hbm, hbm],
        out_specs=[vmem] * 4,
        out_shape=[edge, edge, held, held],
        scratch_shapes=[pltpu.SemaphoreType.DMA((4,))],
        compiler_params=params(12),
        name="edges",
    )(core, in_hbm(x), in_hbm(g))


def faces_kernel(x_ref, g_ref, low_ref, high_ref):
    for s in range(8):
        low_ref[s] = halves(x_ref[s, :, :128], g_ref[s, :, :128], False)
        high_ref[s] = halves(x_ref[s, :, 384:], g_ref[s, :, 384:], True)


def faces(x, g):
    vmem = pl.BlockSpec(memory_space=pltpu.VMEM)
    return pl.pallas_call(
        faces_kernel,
        in_specs=[vmem, vmem],
        out_specs=[vmem, vmem],
        out_shape=[jax.ShapeDtypeStruct((8, 64, 128), BF)] * 2,
        compiler_params=params(8),
        name="faces",
    )(in_vmem(x), in_vmem(g))


def lines_kernel(pair_ref, other_ref, low_ref, high_ref):
    low_ref[...] = halves(pair_ref[:64], other_ref[:64], False)
    high_ref[...] = halves(pair_ref[192:], other_ref[192:], True)


def lines(pair, other):
    vmem = pl.BlockSpec(memory_space=pltpu.VMEM)
    return pl.pallas_call(
        lines_kernel,
        in_specs=[vmem, vmem],
        out_specs=[vmem, vmem],
        out_shape=[jax.ShapeDtypeStruct((64, 128), BF)] * 2,
        compiler_params=params(),
        name="lines",
    )(pair, other)


def weights_kernel(after_ref, blocks_ref, weight_hbm, forward_ref, backward_ref, scale_ref, weight_ref, sem):
    load = pltpu.make_async_copy(weight_hbm, weight_ref, sem)
    load.start()
    active = jnp.sum(jnp.where(blocks_ref[...] >= 0, 1.0, 0.0), axis=0)
    voxels = jnp.sum(jnp.sum(active, axis=1, keepdims=True), axis=0, keepdims=True) * 512.0
    scale_ref[...] = jnp.broadcast_to(1.0 / jnp.sqrt(voxels), (8, 128))
    load.wait()
    rows = iota((128, 128), 0)
    same = jnp.where(rows == iota((128, 128), 1), 1.0, 0.0).astype(BF)
    for k in range(27):
        dz, m = k // 9, k % 9
        forward_ref[64 * m : 64 * m + 64, 64 * dz : 64 * dz + 64] = weight_ref[:, 64 * k : 64 * k + 64]
    for j in range(14):
        wide = min(128, 1728 - 128 * j)
        turned = lax.dot_general(
            same[:wide, :wide],
            weight_ref[:, 128 * j : 128 * j + wide],
            (((1,), (1,)), ((), ())),
            preferred_element_type=F32,
        ).astype(BF)
        for k in range(2 * j, 2 * j + wide // 64):
            dz, m = (26 - k) // 9, (26 - k) % 9
            backward_ref[64 * m : 64 * m + 64, 64 * dz : 64 * dz + 64] = turned[64 * (k - 2 * j) : 64 * (k - 2 * j) + 64]


def arranged_weights(weight, blocks, after):
    vmem = pl.BlockSpec(memory_space=pltpu.VMEM)
    turned = pltpu.VMEM((576, 192), BF)
    return pl.pallas_call(
        weights_kernel,
        in_specs=[pl.BlockSpec(memory_space=pl.ANY), vmem, pl.BlockSpec(memory_space=pltpu.HBM)],
        out_specs=[vmem] * 3,
        out_shape=[turned, turned, jax.ShapeDtypeStruct((8, 128), F32)],
        scratch_shapes=[pltpu.VMEM((64, 1728), BF), pltpu.SemaphoreType.DMA],
        compiler_params=params(),
        name="weights",
    )(after, blocks, in_hbm(weight))


def fill_places(core_ref, table_ref, place_ref):
    odd = core_ref[0]
    lane = iota((8, 128), 1)
    ly = lane // 10 - 1
    lx = lane % 10 - 1
    used = lane < 100
    y_class = jnp.where(ly < 0, 0, jnp.where(ly > 7, 2, 1))
    x_class = jnp.where(lx < 0, 0, jnp.where(lx > 7, 2, 1))
    near = jnp.where(used, y_class * 3 + x_class, -1)
    inner_x = lx & 7
    inner = (ly & 7) * 8 + inner_x
    rows = iota((768, 128), 0)
    for s in range(8):
        r = s // 4
        column = jnp.int32(-10)
        for b in range(8):
            column = jnp.where(table_ref[(4 + r + 1) * 8 + b] == s, b, column)
        for d in range(3):
            source = jnp.full((8, 128), -1, jnp.int32)
            for dy in range(3):
                row = r + dy
                for dx in range(3):
                    at = column + (dx - 1)
                    inside = (at >= 0) & (at < LX)
                    held = table_ref[(d * 4 + row) * 8 + jnp.clip(at, 0, LX - 1)]
                    fine = inside & (held >= 0)
                    if row in (1, 2):
                        base = jnp.where(fine, held * 64, -10000)
                        value = base + inner
                    else:
                        side = 1 - odd if row == 0 else odd
                        base = jnp.where(fine, 512 + side * 128 + (held & 3) * 8, -10000)
                        value = base + inner_x
                    source = jnp.where(near == dy * 3 + dx, value, source)
            place_ref[d, :, 128 * s : 128 * s + 128] = jnp.where(
                rows == source[0:1], 1.0, 0.0
            ).astype(BF)


def places(core, window):
    smem = pl.BlockSpec(memory_space=pltpu.SMEM)
    return pl.pallas_call(
        fill_places,
        in_specs=[smem, smem],
        out_specs=pl.BlockSpec(memory_space=pltpu.VMEM),
        out_shape=pltpu.VMEM((3, 768, 1024), BF),
        compiler_params=params(12),
        name="places",
    )(core, window)


def taps(planes_ref, z_from, z_count):
    return jnp.concatenate(
        [
            jnp.concatenate(
                [planes_ref[64 * (z + dz) : 64 * (z + dz) + 64] for z in range(z_from, z_from + z_count)],
                axis=1,
            )
            for dz in range(3)
        ],
        axis=0,
    )


def terms_kernel(core_ref, place_ref, x_ref, g_ref, below_ref, above_ref, below_line_ref, above_line_ref, pair_ref, other_ref, xa_ref, xb_hbm, ga_hbm, gb_hbm, mine_ref, theirs_ref, left_ref, total_ref, even_ref, odd_ref, xb_ref, ga_ref, gb_ref, sems):
    def fill(row, tiles, right, sides):
        for j in range(4):
            left_ref[row : row + 64, 128 * j : 128 * j + 128] = halves(tiles[2 * j], tiles[2 * j + 1], right)
        for side, (tile, lane_group) in enumerate(sides):
            if lane_group:
                tile = pltpu.roll(tile, 128 - 32 * lane_group, 1)
            left_ref[row : row + 64, 512 + 128 * side : 640 + 128 * side] = tile

    for a, ref in enumerate((x_ref, g_ref)):
        for t in range(4):
            tiles = [ref[s, :, 128 * t : 128 * t + 128] for s in range(8)]
            band = [edge[64 * t : 64 * t + 64] for edge in (pair_ref, other_ref)]
            for parity in range(2):
                fill(512 * a + 64 * (2 * t + parity), tiles, parity, [(tile, 2 * parity + a) for tile in band])
    for side, (ref, line_ref) in enumerate(((below_ref, below_line_ref), (above_ref, above_line_ref))):
        tiles = [ref[s] for s in range(8)]
        line = line_ref[...]
        for a in range(2):
            fill(1024 + 128 * side + 64 * a, tiles, a, [(line, a), (line, 2 + a)])

    x_planes = [(xa_ref, xb_ref)[slot // 4].at[slot % 4] for slot in range(8)]
    g_planes = [(ga_ref, gb_ref)[slot // 4].at[slot % 4] for slot in range(8)]
    for a, planes in enumerate((x_planes, g_planes)):
        main = jnp.dot(
            left_ref[512 * a : 512 * a + 512], place_ref[1], preferred_element_type=F32
        ).astype(BF)
        for slot in range(8):
            planes[slot][64:576] = main[:, 128 * slot : 128 * slot + 128]
    for side in range(2):
        both = jnp.dot(
            left_ref[1024 + 128 * side : 1152 + 128 * side],
            place_ref[2 * side],
            preferred_element_type=F32,
        ).astype(BF)
        for slot in range(8):
            at = slice(128 * slot, 128 * slot + 128)
            x_planes[slot][576 * side : 576 * side + 64] = both[:64, at]
            g_planes[slot][576 * side : 576 * side + 64] = both[64:, at]

    stores = [
        pltpu.make_async_copy(src, dst, sems.at[i])
        for i, (src, dst) in enumerate(((xb_ref, xb_hbm), (ga_ref, ga_hbm), (gb_ref, gb_hbm)))
    ]
    for store in stores:
        store.start()
    total_ref[...] = jnp.zeros_like(total_ref)
    lane = iota((64, 128), 1)
    column = lane % 10
    inner = (lane >= 10) & (lane < 90) & (column >= 1) & (column <= 8)

    def move(slot, moved_ref):
        for z in range(8):
            own = jnp.where(inner, g_planes[slot][64 * (z + 1) : 64 * (z + 1) + 64], jnp.zeros((), BF))
            for m, shift in enumerate(SHIFTS):
                moved_ref[64 * m : 64 * m + 64, 128 * z : 128 * z + 128] = (
                    pltpu.roll(own, shift % 128, 1) if shift else own
                )

    move(0, even_ref)
    for slot in range(8):
        now, later = (even_ref, odd_ref) if slot % 2 == 0 else (odd_ref, even_ref)
        if slot < 7:
            move(slot + 1, later)
        total_ref[...] += lax.dot_general(
            now[...], taps(x_planes[slot], 0, 8), (((1,), (1,)), ((), ())), preferred_element_type=F32
        )

    def part(k):
        if k == 27:
            return jnp.zeros((64, 64), F32)
        return total_ref[64 * (k % 9) : 64 * (k % 9) + 64, 64 * (k // 9) : 64 * (k // 9) + 64]

    def write(refs):
        for j in range(14):
            at = 64 * (j % 7)
            refs[j // 7][at : at + 64] = jnp.concatenate([part(2 * j), part(2 * j + 1)], axis=1)

    pl.when(core_ref[0] == 0)(lambda: write((mine_ref, theirs_ref)))
    pl.when(core_ref[0] == 1)(lambda: write((theirs_ref, mine_ref)))
    for store in stores:
        store.wait()


def planes_and_terms(core, place, x, g, *halo):
    vmem = pl.BlockSpec(memory_space=pltpu.VMEM)
    return pl.pallas_call(
        terms_kernel,
        in_specs=[pl.BlockSpec(memory_space=pltpu.SMEM)] + [vmem] * 9,
        out_specs=[vmem] + [pl.BlockSpec(memory_space=pltpu.HBM)] * 3 + [vmem] * 2,
        out_shape=[pltpu.VMEM((4, 640, 128), BF)] + [pltpu.HBM((4, 640, 128), BF)] * 3 + [jax.ShapeDtypeStruct((448, 128), F32)] * 2,
        scratch_shapes=[pltpu.VMEM((1280, 768), BF), pltpu.VMEM((576, 192), F32)]
        + [pltpu.VMEM((576, 1024), BF)] * 2
        + [pltpu.VMEM((4, 640, 128), BF)] * 3
        + [pltpu.SemaphoreType.DMA((3,))],
        compiler_params=params(24),
        cost_estimate=pl.CostEstimate(flops=10**10, bytes_accessed=10**7, transcendentals=0),
        name="terms",
    )(core, place, x, g, *halo)


def conv_kernel(half, planes_ref, weight_ref, after_ref, *refs):
    out_hbm, token_ref, even_ref, odd_ref, out_ref, sems = refs[-6:]
    row = iota((256, 128), 0)
    lane = row % 128
    y, x = lane // 10 - 1, lane % 10 - 1
    inner = (y >= 0) & (y < 8) & (x >= 0) & (x < 8)
    pick = jnp.where(
        inner & (iota((256, 128), 1) == (row // 128) * 64 + y * 8 + x), 1.0, 0.0
    ).astype(BF)

    def store(slot):
        return pltpu.make_async_copy(out_ref.at[slot], out_hbm.at[4 * half + slot], sems.at[slot])

    def multiply(slot, parts_ref):
        for zp in range(4):
            parts_ref[:, 256 * zp : 256 * zp + 256] = jnp.dot(
                weight_ref[...], taps(planes_ref.at[slot], 2 * zp, 2), preferred_element_type=F32
            )

    def add(slot, parts_ref):
        for zp in range(4):
            tiles = []
            for h in range(2):
                at = 256 * zp + 128 * h
                total = None
                for m, shift in enumerate(SHIFTS):
                    piece = parts_ref[64 * m : 64 * m + 64, at : at + 128]
                    if shift:
                        piece = pltpu.roll(piece, (-shift) % 128, 1)
                    total = piece if total is None else total + piece
                tiles.append(total.astype(BF))
            out_ref[slot, :, 128 * zp : 128 * zp + 128] = jnp.dot(
                jnp.concatenate(tiles, axis=1), pick, preferred_element_type=F32
            ).astype(BF)

    multiply(0, even_ref)
    for slot in range(4):
        now, later = (even_ref, odd_ref) if slot % 2 == 0 else (odd_ref, even_ref)
        if slot < 3:
            multiply(slot + 1, later)
        add(slot, now)
        store(slot).start()
    for slot in range(4):
        store(slot).wait()
    token_ref[...] = jnp.zeros_like(token_ref)


def conv(planes, weight, half, after, into=None):
    anywhere = pl.BlockSpec(memory_space=pl.ANY)
    vmem = pl.BlockSpec(memory_space=pltpu.VMEM)
    hbm = pl.BlockSpec(memory_space=pltpu.HBM)
    return pl.pallas_call(
        functools.partial(conv_kernel, half),
        in_specs=[vmem, vmem, anywhere] + [hbm] * (into is not None),
        out_specs=[hbm, vmem],
        out_shape=[
            jax.ShapeDtypeStruct((8, 64, 512), BF),
            jax.ShapeDtypeStruct((8, 128), F32),
        ],
        scratch_shapes=[pltpu.VMEM((576, 1024), F32)] * 2
        + [pltpu.VMEM((4, 64, 512), BF), pltpu.SemaphoreType.DMA((4,))],
        input_output_aliases={} if into is None else {3: 0},
        compiler_params=params(16),
        cost_estimate=pl.CostEstimate(flops=3 * 10**9, bytes_accessed=10**6, transcendentals=0),
        name="conv",
    )(in_vmem(planes), in_vmem(weight), after, *([] if into is None else [into]))


def coords(i):
    t = i % 64
    return [i // 64, t // 16, (t // 8) % 2, (t // 2) % 4, t % 2]


AXIS = {"zl": (0, 4), "y": (1, 4), "zh": (2, 2), "x": (3, 4), "c": (4, 2)}


def shift_pairs(key, by):
    at, size = AXIS[key]
    out = []
    for i in range(N_DEV):
        v = coords(i)
        v[at] = (v[at] + by) % size
        out.append((i, v[0] * 64 + ((v[1] * 2 + v[2]) * 4 + v[3]) * 2 + v[4]))
    return out


def send(x, key, by):
    return lax.ppermute(x, AXES, shift_pairs(key, by))


def swap_along_z(x, partner):
    pairs = []
    for i in range(N_DEV):
        v = coords(i)
        z = partner[v[2] * 4 + v[0]]
        pairs.append((i, z % 4 * 64 + ((v[1] * 2 + z // 4) * 4 + v[3]) * 2 + v[4]))
    return lax.ppermute(x, AXES, pairs)


def plus(terms, token=None):
    vmem = pl.BlockSpec(memory_space=pltpu.VMEM)
    tokens = [] if token is None else [token]

    def kernel(*refs):
        *parts, out_ref = refs[len(tokens) :]
        out_ref[...] = functools.reduce(jnp.add, [ref[...] for ref in parts])

    return pl.pallas_call(
        kernel,
        in_specs=[pl.BlockSpec(memory_space=pl.ANY)] * len(tokens) + [vmem] * len(terms),
        out_specs=vmem,
        out_shape=jax.ShapeDtypeStruct(terms[0].shape, F32),
        compiler_params=params(),
        name="plus",
    )(*tokens, *terms)


def cut_kernel(me_ref, mine_ref, got_ref, *refs):
    *out_refs, total_ref = refs
    total_ref[...] = mine_ref[...] + got_ref[...]
    for s, ref in enumerate(out_refs):
        at = lax.rem(me_ref[0] + s, 4) * 112
        ref[...] = total_ref[pl.ds(pl.multiple_of(at, 8), 112)]


def cut(me, mine, got):
    vmem = pl.BlockSpec(memory_space=pltpu.VMEM)
    return pl.pallas_call(
        cut_kernel,
        in_specs=[pl.BlockSpec(memory_space=pltpu.SMEM), vmem, vmem],
        out_specs=[vmem] * 4,
        out_shape=[jax.ShapeDtypeStruct((112, 128), F32)] * 4,
        scratch_shapes=[pltpu.VMEM((448, 128), F32)],
        compiler_params=params(),
        name="cut",
    )(me, mine, got)


def assemble_kernel(me_ref, token_ref, *refs):
    *parts, out_ref = refs
    rows = parts[0].shape[0]
    for s, ref in enumerate(parts):
        at = lax.rem(me_ref[0] + s, len(parts)) * rows
        out_ref[pl.ds(pl.multiple_of(at, 8), rows)] = ref[...]


def assemble(me, parts, token):
    vmem = pl.BlockSpec(memory_space=pltpu.VMEM)
    rows = parts[0].shape[0]
    return pl.pallas_call(
        assemble_kernel,
        in_specs=[pl.BlockSpec(memory_space=pltpu.SMEM), pl.BlockSpec(memory_space=pl.ANY)] + [vmem] * len(parts),
        out_specs=vmem,
        out_shape=jax.ShapeDtypeStruct((rows * len(parts), 128), F32),
        compiler_params=params(),
        name="assemble",
    )(me, token, *parts)


def finish_kernel(me_ref, scale_ref, mine_ref, other_ref, out_ref):
    def fill(parts):
        for j in range(14):
            wide = 64 if j == 13 else 128
            out_ref[:, 128 * j : 128 * j + wide] = (
                parts[j // 7][64 * (j % 7) : 64 * (j % 7) + 64, :wide] * scale_ref[0:1, :wide]
            )

    pl.when(me_ref[0] == 0)(lambda: fill((mine_ref, other_ref)))
    pl.when(me_ref[0] == 1)(lambda: fill((other_ref, mine_ref)))


def finish(me, scale, mine, other):
    vmem = pl.BlockSpec(memory_space=pltpu.VMEM)
    return pl.pallas_call(
        finish_kernel,
        in_specs=[pl.BlockSpec(memory_space=pltpu.SMEM)] + [vmem] * 3,
        out_specs=vmem,
        out_shape=jax.ShapeDtypeStruct((64, 1728), F32),
        compiler_params=params(),
        name="finish",
    )(me, scale, mine, other)


def shards(features, cotangent, weight, block_table):
    slab = lax.axis_index("slab")
    tile = lax.axis_index("tile")
    core = (tile % 2).astype(jnp.int32).reshape(1)
    table = jnp.pad(block_table, ((1, 1), (1, 1), (0, 0)), constant_values=-1)
    window = lax.dynamic_slice(table, (slab, tile * YR, 0), (3, 4, LX)).reshape(96)
    to_pair, to_other, x_held, g_held = edges(core, features, cotangent)
    swaps = [(i, i + 1) for i in range(1, 63, 2)]
    other = lax.ppermute(to_other, "tile", swaps + [(b, a) for a, b in swaps])
    pair = lax.ppermute(to_pair, "tile", [(i, i ^ 1) for i in range(64)])
    rise, fall = [(0, 1), (1, 2), (2, 3)], [(1, 0), (2, 1), (3, 2)]
    low, high = faces(x_held, g_held)
    below = lax.ppermute(high, "slab", rise)
    above = lax.ppermute(low, "slab", fall)
    low_line, high_line = lines(pair, other)
    below_line = lax.ppermute(high_line, "slab", rise)
    above_line = lax.ppermute(low_line, "slab", fall)
    place = places(core, window)

    xa, xb, ga, gb, mine, theirs = planes_and_terms(
        core, place, x_held, g_held, below, above, below_line, above_line, pair, other
    )

    x = ((tile // 2) % 4).astype(jnp.int32).reshape(1)
    quarters = cut(x, mine, send(theirs, "c", 1))
    part = quarters[0]

    got = [send(quarters[s], "x", s) for s in (2, 3, 1)]
    forward, backward, scale = arranged_weights(weight, block_table, part)
    part = plus([part] + got, scale)

    got = [send(part, "y", s) for s in (2, 3, 1)]
    conv_out, token = conv(xa, forward, 0, part)
    part = plus([part] + got, token)

    part = plus([part, swap_along_z(part, (1, 0, 3, 2, 5, 4, 7, 6))])

    got = swap_along_z(part, (7, 2, 1, 4, 3, 6, 5, 0))
    conv_out, token = conv(xb, forward, 1, part, conv_out)
    part = plus([part, got], token)

    got = swap_along_z(part, (3, 6, 5, 0, 7, 2, 1, 4))
    grad_features, token = conv(ga, backward, 0, part)
    part = plus([part, got], token)

    got = [send(part, "x", -s) for s in (1, 2, 3)]
    grad_features, token = conv(gb, backward, 1, part, grad_features)
    half = assemble(x, [part] + got, token)

    grad_weight = finish(core, scale, half, send(half, "c", 1))
    return conv_out, grad_features, grad_weight


def solution(mesh):
    rows = P(AXES, None, None)
    return jax.shard_map(
        shards,
        mesh=mesh,
        in_specs=(rows, rows, P(), P()),
        out_specs=(rows, rows, P()),
        check_vma=False,
    )
```
